32 devices in a mesh: req: 4 (over z), tile: 2 (over y), span: 4 (over x, core).
Axes of the slice: x: 2, y: 2, z: 4, core: 2. Of those that a mesh axis runs over, the one named last changes fastest.
Arguments:
- latents: bfloat16 [32, 16, 128, 512], P(('req', 'span'), 'tile'), may hold values from -12 to 12
- frame_counts: int32 [4], replicated, may hold values from 1 to 16, 32 in all
- norm_gain: float32 [512], replicated, may hold values from 0.1 to 1.9
- norm_shift: float32 [512], replicated, may hold values from -3 to 3
- conv_weight: bfloat16 [3, 3, 3, 512, 512], replicated, may hold values from -0.0546875 to 0.0546875
- conv_bias: float32 [512], replicated, may hold values from -2 to 2
Outputs:
- decoded: bfloat16 [32, 16, 128, 512], P(('req', 'span'), 'tile')
The draws below stay inside these ranges and needn't reach their ends.
Inputs may be any that keep to these rules, and one draw needn't show every extreme that they name: `frame_counts`: the 4 counts sum to 32, and the largest is exactly 16.
All inputs are finite; a program needn't handle non-finite values.
Results may differ from the reference program's by a relative error of at most 0.0031.
Values may be sent and summed in bfloat16 or wider, within the bound.
A program may use at most 192 MiB of HBM per device.

```python
import math
import jax
import jax.numpy as jnp
import numpy as np
from jax import lax

C = 512
GROUPS = 32
REQS = 4
W = 128
FRAMES = 32
ROWS = 16


def draw_latents(key, part):
    noise_key, scale_key = jax.random.split(jax.random.fold_in(key, 17), 2)
    noise = jax.random.normal(noise_key, (FRAMES, ROWS, W, C), jnp.float32)
    frame_rise = (jnp.arange(FRAMES, dtype=jnp.float32) / max(FRAMES - 1, 1)).reshape(FRAMES, 1, 1, 1)
    row_rise = (jnp.arange(ROWS, dtype=jnp.float32) / max(ROWS - 1, 1)).reshape(1, ROWS, 1, 1)
    jitter = jax.random.uniform(scale_key, (FRAMES, ROWS, 1, 1), jnp.float32, 0.8, 1.25)
    scale = 0.6 * jnp.exp(0.5 * math.log(3.0) * (frame_rise + row_rise)) * jitter
    return jnp.clip(scale * noise, -12.0, 12.0).astype(jnp.bfloat16)


def profile(amount, total, limit, skew):
    portions = [(1 << 20) // math.isqrt(standing ** skew) + 1 for standing in range(2, amount + 1)]
    spare, holding = total - limit - (amount - 1), [1] * (amount - 1)
    while spare > 0:
        candidates = [i for i in range(amount - 1) if holding[i] < limit]
        whole, remaining = sum([portions[i] for i in candidates]), spare
        for i in candidates:
            more = min(limit - holding[i], max(1, remaining * portions[i] // whole), spare)
            holding[i] = holding[i] + more
            spare = spare - more
    return np.array([limit] + holding)


def ragged_sizes(key, amount, total, most, slope):
    if amount == 2:
        one = jax.random.randint(key, (), max(1, total - most), min(most, total - 1) + 1)
        return jnp.stack([one, total - one])
    tallies = jnp.asarray(profile(amount, total, most, slope), jnp.int32)
    pairs = (amount - 1) // 2
    giver, receiver = tallies[1:1 + 2 * pairs:2], tallies[2:2 + 2 * pairs:2]
    room = jnp.minimum(giver - 1, most - receiver)
    moved = jax.random.randint(jax.random.fold_in(key, 1), (pairs,), 0, 1 << 20) % (room + 1)
    tallies = tallies.at[1:1 + 2 * pairs:2].set(giver - moved).at[2:2 + 2 * pairs:2].set(receiver + moved)
    return tallies[jax.random.permutation(jax.random.fold_in(key, 2), amount)]


def scatter_about(key, extent, scale, most, kind=jnp.bfloat16):
    entries = scale * jax.random.normal(key, extent, jnp.float32)
    return jnp.clip(entries, min=-most, max=most).astype(kind)


def setup_inputs(seed: int = 0) -> dict:
    key_of = jax.random.split(jax.random.key(seed), 7)
    latents = draw_latents(jax.random.fold_in(key_of[6], 71), 0)
    frame_counts = ragged_sizes(key_of[1], REQS, FRAMES, FRAMES // 2, 2).astype(jnp.int32)
    norm_gain = jnp.clip(1.0 + 0.18 * jax.random.normal(key_of[2], (C,), jnp.float32), 0.1, 1.9)
    norm_shift = scatter_about(key_of[3], (C,), 0.5, 3.0, jnp.float32)
    conv_weight = scatter_about(key_of[4], (3, 3, 3, C, C), (27 * C) ** -0.5, 0.0546875)
    conv_bias = scatter_about(key_of[5], (C,), 0.3, 2.0, jnp.float32)
    return dict(latents=latents, frame_counts=frame_counts, norm_gain=norm_gain, norm_shift=norm_shift, conv_weight=conv_weight, conv_bias=conv_bias)


EPSILON = 1e-06

def membership(positions, request_start, request_end):
    return (positions[:, None] >= request_start[None, :]) & (positions[:, None] < request_end[None, :])

def normalize(source, positions, request_start, request_end, group_mean, group_scale, norm_gain, norm_shift):
    inside = membership(positions, request_start, request_end).astype(jnp.float32)
    per_group = source.shape[-1] // group_mean.shape[1]
    frame_mean = jnp.repeat(jnp.dot(inside, group_mean, precision=lax.Precision.HIGHEST), per_group, axis=1)
    frame_scale = jnp.repeat(jnp.dot(inside, group_scale, precision=lax.Precision.HIGHEST), per_group, axis=1)
    centred = (source.astype(jnp.float32) - frame_mean[:, None, None, :]) * frame_scale[:, None, None, :]
    return jax.nn.silu(centred * norm_gain + norm_shift).astype(jnp.bfloat16)

def reference(latents, frame_counts, norm_gain, norm_shift, conv_weight, conv_bias):
    frame_count, row_count, col_count, channels = latents.shape
    per_group = channels // GROUPS
    request_end = jnp.cumsum(frame_counts).astype(jnp.int32)
    request_start = (request_end - frame_counts).astype(jnp.int32)
    positions = jnp.arange(frame_count, dtype=jnp.int32)
    inside = membership(positions, request_start, request_end)
    values = latents.astype(jnp.float32)
    group_sums = lax.optimization_barrier(jnp.sum(values, axis=(1, 2))).reshape(frame_count, GROUPS, per_group).sum(-1)
    group_squares = lax.optimization_barrier(jnp.sum(values * values, axis=(1, 2))).reshape(frame_count, GROUPS, per_group).sum(-1)
    weights_in = inside.astype(jnp.float32)
    total_sums = jnp.dot(weights_in.T, group_sums, precision=lax.Precision.HIGHEST)
    total_squares = jnp.dot(weights_in.T, group_squares, precision=lax.Precision.HIGHEST)
    cell_count = (frame_counts * (row_count * col_count * per_group)).astype(jnp.float32)[:, None]
    group_mean = total_sums / cell_count
    group_scale = lax.rsqrt(total_squares / cell_count - group_mean * group_mean + EPSILON)
    hidden = normalize(latents, positions, request_start, request_end, group_mean, group_scale, norm_gain, norm_shift)
    padded = jnp.pad(hidden, ((0, 0), (1, 1), (1, 1), (0, 0)), mode='edge')
    frame_start = lax.optimization_barrier(jnp.sum(jnp.where(inside, request_start[None, :], 0), axis=1)).astype(jnp.int32)
    tap_index = jnp.stack([jnp.maximum(positions - 2 + time_tap, frame_start) for time_tap in range(3)], axis=1)

    def one_frame(frame_taps):
        accumulated = jnp.zeros((row_count * col_count, channels), jnp.float32)
        for time_tap in range(3):
            chosen = jnp.take(padded, frame_taps[time_tap], axis=0)
            for row_tap in range(3):
                stacked = jnp.concatenate([chosen[row_tap:row_tap + row_count, col_tap:col_tap + col_count] for col_tap in range(3)], axis=-1)
                kernel = conv_weight[time_tap, row_tap].reshape(3 * channels, channels)
                accumulated = accumulated + jnp.dot(stacked.reshape(row_count * col_count, 3 * channels), kernel, preferred_element_type=jnp.float32)
        return accumulated.reshape(row_count, col_count, channels)
    conv = lax.map(one_frame, tap_index)
    return (values + conv + conv_bias).astype(jnp.bfloat16)
```

```python
import functools

import jax
import jax.numpy as jnp
from jax import lax
from jax.experimental import pallas as pl
from jax.experimental.pallas import tpu as pltpu
from jax.sharding import PartitionSpec as P

GROUPS = 32
EPSILON = 1e-06
MESH = pl.DeviceIdType.MESH
HIGHEST = lax.Precision.HIGHEST
F32 = jnp.float32


def kernel(
    sizes,
    counts,
    lat,
    gain,
    shift,
    bias,
    weight,
    out,
    own,
    prev,
    rim,
    wv,
    hid,
    acc,
    msg,
    stat_a,
    stat_b,
    table,
    own_sem,
    w_sem,
    out_sem,
    a_send,
    a_recv,
    b_send,
    b_recv,
    rim_send,
    rim_recv,
    frame_send,
    frame_recv,
):
    reqs_n, tiles, spans = sizes
    frames, rows, cols, channels = own.shape
    per_group = channels // GROUPS
    requests = counts.shape[0]
    req, tile, span = (lax.axis_index("req"), lax.axis_index("tile"), lax.axis_index("span"))
    place = req * spans + span
    places = reqs_n * spans
    has_next, has_prev = place < places - 1, place > 0
    has_up, has_down = tile > 0, tile < tiles - 1

    def at(chain, row):
        return {"req": chain // spans, "tile": row, "span": chain % spans}

    def chain_to(by):
        return jnp.clip(place + by, 0, places - 1)

    members_a = tiles * spans
    me_a = tile * spans + span

    def partner_a(k):
        other = (me_a + k) % members_a
        return {"req": req, "tile": other // spans, "span": other % spans}

    def partner_b(k):
        return {"req": (req + k) % reqs_n, "tile": tile, "span": span}

    for f in range(frames):
        pltpu.make_async_copy(lat.at[f], own.at[f], own_sem.at[f]).start()

    barrier = pltpu.get_barrier_semaphore()
    for k in range(1, members_a):
        pl.semaphore_signal(barrier, inc=1, device_id=partner_a(k), device_id_type=MESH)
    for k in range(1, reqs_n):
        pl.semaphore_signal(barrier, inc=1, device_id=partner_b(k), device_id_type=MESH)
    for by, has in ((1, has_next), (-1, has_prev)):

        @pl.when(has)
        def _():
            pl.semaphore_signal(
                barrier, inc=1, device_id=at(chain_to(by), tile), device_id_type=MESH
            )

        for step, has_row in ((-1, has_up), (1, has_down)):

            @pl.when(has & has_row)
            def _():
                pl.semaphore_signal(
                    barrier,
                    inc=1,
                    device_id=at(chain_to(by), jnp.clip(tile + step, 0, tiles - 1)),
                    device_id_type=MESH,
                )

    for t in (2, 1, 0):
        for b in range(3):
            i = 3 * t + b
            pltpu.make_async_copy(weight.at[i], wv.at[i], w_sem.at[i]).start()

    start_of, end_of, total = [], [], jnp.int32(0)
    for r in range(requests):
        start_of.append(total)
        total = total + counts[r]
        end_of.append(total)
    first = place * frames

    def member(slot, r):
        position = first + slot - 2
        return (position >= start_of[r]) & (position < end_of[r])

    def start_at(slot):
        found = jnp.int32(0)
        for r in range(requests):
            found = jnp.where(member(slot, r), start_of[r], found)
        return found

    per_frame = []
    for f in range(frames):
        pltpu.make_async_copy(lat.at[f], own.at[f], own_sem.at[f]).wait()

        def add_row(i, carry):
            s, q = carry
            x = own[f, i].astype(F32).reshape(cols // 8, 8, channels)
            return (s + jnp.sum(x, axis=0), q + jnp.sum(x * x, axis=0))

        zero = jnp.zeros((8, channels), F32)
        s, q = lax.fori_loop(0, rows, add_row, (zero, zero))
        per_frame.append((jnp.sum(s, axis=0, keepdims=True), jnp.sum(q, axis=0, keepdims=True)))
    table[...] = jnp.zeros_like(table)
    for r in range(requests):
        for which in range(2):
            line = jnp.zeros((1, channels), F32)
            for f in range(frames):
                line = line + jnp.where(member(f + 2, r), per_frame[f][which], 0.0)
            table[which * requests + r : which * requests + r + 1, :] = line
    lanes = msg.shape[1]
    to_group = (
        lax.broadcasted_iota(jnp.int32, (channels, lanes), 0) // per_group
        == lax.broadcasted_iota(jnp.int32, (channels, lanes), 1)
    ).astype(F32)
    from_group = (
        lax.broadcasted_iota(jnp.int32, (lanes, channels), 1) // per_group
        == lax.broadcasted_iota(jnp.int32, (lanes, channels), 0)
    ).astype(F32)
    msg[...] = jnp.dot(table[...], to_group, precision=HIGHEST, preferred_element_type=F32)
    stat_a[me_a] = msg[...]

    near = has_up.astype(jnp.int32) + has_down.astype(jnp.int32)
    sides = has_next.astype(jnp.int32) + has_prev.astype(jnp.int32)
    pl.semaphore_wait(barrier, members_a - 1 + reqs_n - 1 + sides * (1 + near))

    def copy_a(k):
        return pltpu.make_async_remote_copy(
            src_ref=msg,
            dst_ref=stat_a.at[me_a],
            send_sem=a_send.at[k],
            recv_sem=a_recv.at[me_a],
            device_id=partner_a(k),
            device_id_type=MESH,
        )

    def copy_b(k):
        return pltpu.make_async_remote_copy(
            src_ref=table.at[:, 0:lanes],
            dst_ref=stat_b.at[req],
            send_sem=b_send.at[k],
            recv_sem=b_recv.at[req],
            device_id=partner_b(k),
            device_id_type=MESH,
        )

    def rim_copy(slot, side):
        edge = rows - 1 if side == 0 else 0
        row_to = jnp.clip(tile + (1 if side == 0 else -1), 0, tiles - 1)
        forward = slot == 0
        source = lat.at[frames - 2 : frames, edge] if forward else lat.at[:, edge]
        count = 2 if forward else frames
        return pltpu.make_async_remote_copy(
            src_ref=source,
            dst_ref=rim.at[side, slot : slot + count],
            send_sem=rim_send.at[side, slot // 2],
            recv_sem=rim_recv.at[side, slot // 2],
            device_id=at(chain_to(1) if forward else place, row_to),
            device_id_type=MESH,
        )

    def frame_copy(slot):
        return pltpu.make_async_remote_copy(
            src_ref=lat.at[frames - 2 + slot],
            dst_ref=prev.at[slot],
            send_sem=frame_send.at[slot],
            recv_sem=frame_recv.at[slot],
            device_id=at(chain_to(1), tile),
            device_id_type=MESH,
        )

    row_sends = ((0, has_down), (1, has_up))
    row_recvs = ((0, has_up), (1, has_down))

    for k in range(1, members_a):
        copy_a(k).start()
    for side, has in row_sends:
        pl.when(has)(lambda side=side: rim_copy(2, side).start())
    pl.when(has_next)(lambda: frame_copy(1).start())

    for k in range(1, members_a):
        copy_a(k).wait_send()
        other = (me_a + k) % members_a
        pltpu.make_async_remote_copy(
            src_ref=msg,
            dst_ref=stat_a.at[other],
            send_sem=a_send.at[k],
            recv_sem=a_recv.at[other],
            device_id=partner_a(k),
            device_id_type=MESH,
        ).wait_recv()
    part = jnp.sum(stat_a[...], axis=0)
    table[:, 0:lanes] = part
    stat_b[req] = part
    for k in range(1, reqs_n):
        copy_b(k).start()
    for side, has in row_sends:
        pl.when(has & has_next)(lambda side=side: rim_copy(0, side).start())
    pl.when(has_next)(lambda: frame_copy(0).start())
    for k in range(1, reqs_n):
        copy_b(k).wait_send()
        other = (req + k) % reqs_n
        pltpu.make_async_remote_copy(
            src_ref=table.at[:, 0:lanes],
            dst_ref=stat_b.at[other],
            send_sem=b_send.at[k],
            recv_sem=b_recv.at[other],
            device_id=partner_b(k),
            device_id_type=MESH,
        ).wait_recv()
    whole = jnp.sum(stat_b[...], axis=0)
    cells = rows * tiles * cols * per_group
    lines = []
    for r in range(requests):
        n = jnp.full((1, lanes), counts[r] * cells, jnp.int32).astype(F32)
        mean = whole[r : r + 1] / n
        scale = lax.rsqrt(whole[requests + r : requests + r + 1] / n - mean * mean + EPSILON)
        lines.append((mean, scale))
    for r in range(requests):
        msg[r : r + 1, :] = lines[r][0]
        msg[requests + r : requests + r + 1, :] = lines[r][1]
    table[...] = jnp.dot(msg[...], from_group, precision=HIGHEST, preferred_element_type=F32)

    lane = min(128, channels)
    first_col = lax.broadcasted_iota(jnp.int32, (cols, lane), 0) == 0
    last_col = lax.broadcasted_iota(jnp.int32, (cols, lane), 0) == cols - 1

    def coefficients(slot):
        mean = jnp.zeros((1, channels), F32)
        scale = jnp.zeros((1, channels), F32)
        for r in range(requests):
            inside = member(slot, r)
            mean = jnp.where(inside, table[r : r + 1, :], mean)
            scale = jnp.where(inside, table[requests + r : requests + r + 1, :], scale)
        return mean, scale * gain[...] * 0.5, shift[...] * 0.5

    def put_row(slot, row, read, coef):
        mean, factor, offset = coef
        for c in range(0, channels, lane):
            part = slice(c, c + lane)
            x = read(part).astype(F32)
            h = (x - mean[:, part]) * factor[:, part] + offset[:, part]
            y = h + h * jnp.tanh(h)
            left = jnp.where(first_col, y, pltpu.roll(y, 1, 0))
            right = jnp.where(last_col, y, pltpu.roll(y, cols - 1, 0))
            hid[slot, row, :, c : c + lane] = left.astype(jnp.bfloat16)
            hid[slot, row, :, channels + c : channels + c + lane] = y.astype(jnp.bfloat16)
            hid[slot, row, :, 2 * channels + c : 2 * channels + c + lane] = right.astype(
                jnp.bfloat16
            )

    def put_frame(slot, source, index):
        coef = coefficients(slot)

        def body(i, _):
            put_row(slot, i + 1, lambda part: source[index, i, :, part], coef)
            return 0

        lax.fori_loop(0, rows, body, 0)
        for side, has in row_recvs:
            row = 0 if side == 0 else rows + 1
            edge = 0 if side == 0 else rows - 1

            @pl.when(has)
            def _():
                put_row(slot, row, lambda part: rim[side, slot, :, part], coef)

            @pl.when(jnp.logical_not(has))
            def _():
                hid[slot, row] = hid[slot, 1 + edge]

    def multiply(f, t, begin, end):
        source = jnp.maximum(first + f - 2 + t, start_at(f + 2)) - first + 2

        def body(b, _):
            if begin:
                i = 3 * t + b
                pltpu.make_async_copy(weight.at[i], wv.at[i], w_sem.at[i]).wait()
            lhs = hid[source, pl.ds(b, rows)].reshape(rows * cols, 3 * channels)
            acc[f] += jnp.dot(lhs, wv[3 * t + b], preferred_element_type=F32)
            return 0

        lax.fori_loop(0, 3, body, 0)
        if end:
            value = own[f].reshape(rows * cols, channels).astype(F32) + acc[f] + bias[...]
            own[f] = value.astype(jnp.bfloat16).reshape(rows, cols, channels)
            pltpu.make_async_copy(own.at[f], out.at[f], out_sem.at[f]).start()

    for side, has in row_recvs:
        pl.when(has)(lambda side=side: rim_copy(2, side).wait_recv())
    for f in range(frames):
        put_frame(f + 2, own, f)
    acc[...] = jnp.zeros_like(acc)

    pairs = [(f, t) for f in range(frames) for t in (2, 1, 0)]
    order = sorted(pairs, key=lambda p: (max(0, 2 - p[0] - p[1]), -p[1], -p[0]))
    seen, left = set(), {f: 3 for f in range(frames)}
    ready = 0
    for f, t in order:
        need = max(0, 2 - f - t)
        while ready < need:
            ready += 1
            slot = 2 - ready

            @pl.when(has_prev)
            def _():
                frame_copy(slot).wait_recv()
                if ready == 1:
                    for side, has in row_recvs:
                        pl.when(has)(lambda side=side: rim_copy(0, side).wait_recv())
                put_frame(slot, prev, slot)

        left[f] -= 1
        multiply(f, t, t not in seen, left[f] == 0)
        seen.add(t)

    for side, has in row_sends:
        pl.when(has)(lambda side=side: rim_copy(2, side).wait_send())
        pl.when(has & has_next)(lambda side=side: rim_copy(0, side).wait_send())
    for slot in range(2):
        pl.when(has_next)(lambda slot=slot: frame_copy(slot).wait_send())
    for f in range(frames):
        pltpu.make_async_copy(own.at[f], out.at[f], out_sem.at[f]).wait()


def solution(mesh):
    sizes = (mesh.shape["req"], mesh.shape["tile"], mesh.shape["span"])
    reqs_n, tiles, spans = sizes

    def step(latents, frame_counts, norm_gain, norm_shift, conv_weight, conv_bias):
        frames, rows, cols, channels = latents.shape
        taps = conv_weight.shape[1] * conv_weight.shape[2]
        lines = -(-2 * frame_counts.shape[0] // 8) * 8
        members = tiles * spans
        bf16, dma = jnp.bfloat16, pltpu.SemaphoreType.DMA
        weight = conv_weight.reshape(9, 3 * channels, channels)
        whole = pl.BlockSpec(memory_space=pltpu.VMEM)
        anywhere = pl.BlockSpec(memory_space=pl.ANY)
        positions = frames * rows * cols
        return pl.pallas_call(
            functools.partial(kernel, sizes),
            out_shape=jax.ShapeDtypeStruct(latents.shape, bf16),
            in_specs=[
                pl.BlockSpec(memory_space=pltpu.SMEM),
                anywhere,
                whole,
                whole,
                whole,
                anywhere,
            ],
            out_specs=anywhere,
            scratch_shapes=[
                pltpu.VMEM((frames, rows, cols, channels), bf16),
                pltpu.VMEM((2, rows, cols, channels), bf16),
                pltpu.VMEM((2, frames + 2, cols, channels), bf16),
                pltpu.VMEM((9, 3 * channels, channels), bf16),
                pltpu.VMEM((frames + 2, rows + 2, cols, 3 * channels), bf16),
                pltpu.VMEM((frames, rows * cols, channels), F32),
                pltpu.VMEM((lines, 128), F32),
                pltpu.VMEM((members, lines, 128), F32),
                pltpu.VMEM((reqs_n, lines, 128), F32),
                pltpu.VMEM((lines, channels), F32),
                dma((frames,)),
                dma((9,)),
                dma((frames,)),
                dma((members,)),
                dma((members,)),
                dma((reqs_n,)),
                dma((reqs_n,)),
                dma((2, 2)),
                dma((2, 2)),
                dma((2,)),
                dma((2,)),
            ],
            compiler_params=pltpu.CompilerParams(
                collective_id=0, has_side_effects=True, vmem_limit_bytes=56 * 1024 * 1024
            ),
            cost_estimate=pl.CostEstimate(
                flops=2 * positions * 3 * taps * channels * channels,
                bytes_accessed=2 * 3 * taps * channels * channels + 4 * positions * channels,
                transcendentals=2 * positions * channels,
            ),
        )(
            frame_counts,
            latents,
            norm_gain.reshape(1, channels),
            norm_shift.reshape(1, channels),
            conv_bias.reshape(1, channels),
            weight,
        )

    placed = (P(("req", "span"), "tile", None, None), P(), P(), P(), P(), P())
    return jax.shard_map(
        step,
        mesh=mesh,
        in_specs=placed,
        out_specs=P(("req", "span"), "tile", None, None),
        check_vma=False,
    )
```

```python
import functools

import jax
import jax.numpy as jnp
from jax import lax
from jax.experimental import pallas as pl
from jax.experimental.pallas import tpu as pltpu
from jax.sharding import PartitionSpec as P

GROUPS = 32
EPSILON = 1e-06
MESH = pl.DeviceIdType.MESH
HIGHEST = lax.Precision.HIGHEST
F32 = jnp.float32


def kernel(
    sizes,
    counts,
    lat,
    gain,
    shift,
    bias,
    weight,
    out,
    own,
    prev,
    rim,
    wv,
    line_buf,
    hid,
    acc,
    msg,
    stat_a,
    stat_b,
    table,
    own_sem,
    w_sem,
    out_sem,
    a_send,
    a_recv,
    b_send,
    b_recv,
    rim_send,
    rim_recv,
    frame_send,
    frame_recv,
):
    reqs_n, tiles, spans = sizes
    frames, rows, cols, channels = own.shape
    per_group = channels // GROUPS
    requests = counts.shape[0]
    req, tile, span = (lax.axis_index("req"), lax.axis_index("tile"), lax.axis_index("span"))
    place = req * spans + span
    places = reqs_n * spans
    has_next, has_prev = place < places - 1, place > 0
    has_up, has_down = tile > 0, tile < tiles - 1

    def at(chain, row):
        return {"req": chain // spans, "tile": row, "span": chain % spans}

    def chain_to(by):
        return jnp.clip(place + by, 0, places - 1)

    members_a = tiles * spans
    me_a = tile * spans + span

    def partner_a(k):
        other = (me_a + k) % members_a
        return {"req": req, "tile": other // spans, "span": other % spans}

    def partner_b(k):
        return {"req": (req + k) % reqs_n, "tile": tile, "span": span}

    for f in range(frames):
        pltpu.make_async_copy(lat.at[f], own.at[f], own_sem.at[f]).start()

    barrier = pltpu.get_barrier_semaphore()
    for k in range(1, members_a):
        pl.semaphore_signal(barrier, inc=1, device_id=partner_a(k), device_id_type=MESH)
    for k in range(1, reqs_n):
        pl.semaphore_signal(barrier, inc=1, device_id=partner_b(k), device_id_type=MESH)
    for by, has in ((1, has_next), (-1, has_prev)):

        @pl.when(has)
        def _():
            pl.semaphore_signal(
                barrier, inc=1, device_id=at(chain_to(by), tile), device_id_type=MESH
            )

        for step, has_row in ((-1, has_up), (1, has_down)):

            @pl.when(has & has_row)
            def _():
                pl.semaphore_signal(
                    barrier,
                    inc=1,
                    device_id=at(chain_to(by), jnp.clip(tile + step, 0, tiles - 1)),
                    device_id_type=MESH,
                )

    def weight_copy(t, b):
        return pltpu.make_async_copy(
            weight.at[3 * t + b], wv.at[4 * t + (0, 1, 3)[b]], w_sem.at[3 * t + b]
        )

    def blend_weights(t):
        for b in range(3):
            weight_copy(t, b).wait()
        size = 32

        def body(i, _):
            part = pl.ds(pl.multiple_of(i * size, size), size)
            outer = wv[4 * t, part].astype(F32) + wv[4 * t + 3, part].astype(F32)
            middle = wv[4 * t + 1, part].astype(F32)
            wv[4 * t + 1, part] = (outer + middle).astype(jnp.bfloat16)
            wv[4 * t + 2, part] = (outer - middle).astype(jnp.bfloat16)
            return 0

        lax.fori_loop(0, wv.shape[1] // size, body, 0)

    for t in (2, 1, 0):
        for b in range(3):
            weight_copy(t, b).start()

    start_of, end_of, total = [], [], jnp.int32(0)
    for r in range(requests):
        start_of.append(total)
        total = total + counts[r]
        end_of.append(total)
    first = place * frames

    def member(slot, r):
        position = first + slot - 2
        return (position >= start_of[r]) & (position < end_of[r])

    def start_at(slot):
        found = jnp.int32(0)
        for r in range(requests):
            found = jnp.where(member(slot, r), start_of[r], found)
        return found

    per_frame = []
    for f in range(frames):
        pltpu.make_async_copy(lat.at[f], own.at[f], own_sem.at[f]).wait()

        def add_row(i, carry):
            s, q = carry
            x = own[f, i].astype(F32).reshape(cols // 8, 8, channels)
            return (s + jnp.sum(x, axis=0), q + jnp.sum(x * x, axis=0))

        zero = jnp.zeros((8, channels), F32)
        s, q = lax.fori_loop(0, rows, add_row, (zero, zero))
        per_frame.append((jnp.sum(s, axis=0, keepdims=True), jnp.sum(q, axis=0, keepdims=True)))
    table[...] = jnp.zeros_like(table)
    for r in range(requests):
        for which in range(2):
            line = jnp.zeros((1, channels), F32)
            for f in range(frames):
                line = line + jnp.where(member(f + 2, r), per_frame[f][which], 0.0)
            table[which * requests + r : which * requests + r + 1, :] = line
    lanes = msg.shape[1]
    to_group = (
        lax.broadcasted_iota(jnp.int32, (channels, lanes), 0) // per_group
        == lax.broadcasted_iota(jnp.int32, (channels, lanes), 1)
    ).astype(F32)
    from_group = (
        lax.broadcasted_iota(jnp.int32, (lanes, channels), 1) // per_group
        == lax.broadcasted_iota(jnp.int32, (lanes, channels), 0)
    ).astype(F32)
    msg[...] = jnp.dot(table[...], to_group, precision=HIGHEST, preferred_element_type=F32)
    stat_a[me_a] = msg[...]

    near = has_up.astype(jnp.int32) + has_down.astype(jnp.int32)
    sides = has_next.astype(jnp.int32) + has_prev.astype(jnp.int32)
    pl.semaphore_wait(barrier, members_a - 1 + reqs_n - 1 + sides * (1 + near))

    def copy_a(k):
        return pltpu.make_async_remote_copy(
            src_ref=msg,
            dst_ref=stat_a.at[me_a],
            send_sem=a_send.at[k],
            recv_sem=a_recv.at[me_a],
            device_id=partner_a(k),
            device_id_type=MESH,
        )

    def copy_b(k):
        return pltpu.make_async_remote_copy(
            src_ref=table.at[:, 0:lanes],
            dst_ref=stat_b.at[req],
            send_sem=b_send.at[k],
            recv_sem=b_recv.at[req],
            device_id=partner_b(k),
            device_id_type=MESH,
        )

    def rim_copy(slot, side):
        edge = rows - 1 if side == 0 else 0
        row_to = jnp.clip(tile + (1 if side == 0 else -1), 0, tiles - 1)
        forward = slot == 0
        source = lat.at[frames - 2 : frames, edge] if forward else lat.at[:, edge]
        count = 2 if forward else frames
        return pltpu.make_async_remote_copy(
            src_ref=source,
            dst_ref=rim.at[side, slot : slot + count],
            send_sem=rim_send.at[side, slot // 2],
            recv_sem=rim_recv.at[side, slot // 2],
            device_id=at(chain_to(1) if forward else place, row_to),
            device_id_type=MESH,
        )

    def frame_copy(slot):
        return pltpu.make_async_remote_copy(
            src_ref=lat.at[frames - 2 + slot],
            dst_ref=prev.at[slot],
            send_sem=frame_send.at[slot],
            recv_sem=frame_recv.at[slot],
            device_id=at(chain_to(1), tile),
            device_id_type=MESH,
        )

    row_sends = ((0, has_down), (1, has_up))
    row_recvs = ((0, has_up), (1, has_down))

    for k in range(1, members_a):
        copy_a(k).start()
    for side, has in row_sends:
        pl.when(has)(lambda side=side: rim_copy(2, side).start())
    pl.when(has_next)(lambda: frame_copy(1).start())
    blend_weights(2)

    for k in range(1, members_a):
        copy_a(k).wait_send()
        other = (me_a + k) % members_a
        pltpu.make_async_remote_copy(
            src_ref=msg,
            dst_ref=stat_a.at[other],
            send_sem=a_send.at[k],
            recv_sem=a_recv.at[other],
            device_id=partner_a(k),
            device_id_type=MESH,
        ).wait_recv()
    part = jnp.sum(stat_a[...], axis=0)
    table[:, 0:lanes] = part
    stat_b[req] = part
    for k in range(1, reqs_n):
        copy_b(k).start()
    for side, has in row_sends:
        pl.when(has & has_next)(lambda side=side: rim_copy(0, side).start())
    pl.when(has_next)(lambda: frame_copy(0).start())
    blend_weights(1)
    blend_weights(0)
    for k in range(1, reqs_n):
        copy_b(k).wait_send()
        other = (req + k) % reqs_n
        pltpu.make_async_remote_copy(
            src_ref=table.at[:, 0:lanes],
            dst_ref=stat_b.at[other],
            send_sem=b_send.at[k],
            recv_sem=b_recv.at[other],
            device_id=partner_b(k),
            device_id_type=MESH,
        ).wait_recv()
    whole = jnp.sum(stat_b[...], axis=0)
    cells = rows * tiles * cols * per_group
    lines = []
    for r in range(requests):
        n = jnp.full((1, lanes), counts[r] * cells, jnp.int32).astype(F32)
        mean = whole[r : r + 1] / n
        scale = lax.rsqrt(whole[requests + r : requests + r + 1] / n - mean * mean + EPSILON)
        lines.append((mean, scale))
    for r in range(requests):
        msg[r : r + 1, :] = lines[r][0]
        msg[requests + r : requests + r + 1, :] = lines[r][1]
    table[...] = jnp.dot(msg[...], from_group, precision=HIGHEST, preferred_element_type=F32)

    lane = min(128, channels)
    first_col = lax.broadcasted_iota(jnp.int32, (cols, lane), 0) == 0
    last_col = lax.broadcasted_iota(jnp.int32, (cols, lane), 0) == cols - 1

    def coefficients(slot):
        mean = jnp.zeros((1, channels), F32)
        scale = jnp.zeros((1, channels), F32)
        for r in range(requests):
            inside = member(slot, r)
            mean = jnp.where(inside, table[r : r + 1, :], mean)
            scale = jnp.where(inside, table[requests + r : requests + r + 1, :], scale)
        return mean, scale * gain[...] * 0.5, shift[...] * 0.5

    def put_row(row, read, coef):
        mean, factor, offset = coef
        for c in range(0, channels, lane):
            part = slice(c, c + lane)
            x = read(part).astype(F32)
            h = (x - mean[:, part]) * factor[:, part] + offset[:, part]
            y = h + h * jnp.tanh(h)
            left = jnp.where(first_col, y, pltpu.roll(y, 1, 0))
            right = jnp.where(last_col, y, pltpu.roll(y, cols - 1, 0))
            line_buf[row, :, c : c + lane] = left.astype(jnp.bfloat16)
            line_buf[row, :, channels + c : channels + c + lane] = y.astype(jnp.bfloat16)
            line_buf[row, :, 2 * channels + c : 2 * channels + c + lane] = right.astype(
                jnp.bfloat16
            )

    def put_frame(slot, source, index):
        coef = coefficients(slot)

        def body(i, _):
            put_row(i + 1, lambda part: source[index, i, :, part], coef)
            return 0

        lax.fori_loop(0, rows, body, 0)
        for side, has in row_recvs:
            row = 0 if side == 0 else rows + 1
            edge = 0 if side == 0 else rows - 1

            @pl.when(has)
            def _():
                put_row(row, lambda part: rim[side, slot, :, part], coef)

            @pl.when(jnp.logical_not(has))
            def _():
                line_buf[row] = line_buf[1 + edge]

        def blend_rows(i, _):
            for c in range(0, 3 * channels, lane):
                part = slice(c, c + lane)
                d0, d1, d2, d3 = [line_buf[2 * i + n, :, part] for n in range(4)]
                hid[slot, 0, i, :, part] = d0 - d2
                hid[slot, 1, i, :, part] = d1 + d2
                hid[slot, 2, i, :, part] = d2 - d1
                hid[slot, 3, i, :, part] = d1 - d3
            return 0

        lax.fori_loop(0, rows // 2, blend_rows, 0)

    def multiply(f, t, begin, end):
        source = jnp.maximum(first + f - 2 + t, start_at(f + 2)) - first + 2

        def body(k, _):
            lhs = hid[source, k].reshape(rows // 2 * cols, 3 * channels)
            term = jnp.dot(lhs, wv[4 * t + k], preferred_element_type=F32)
            acc[f, k] = term if begin else acc[f, k] + term
            return 0

        lax.fori_loop(0, 4, body, 0)
        if end:

            def finish(i, _):
                part = pl.ds(pl.multiple_of(i * cols, cols), cols)
                m0, m1, m2, m3 = [acc[f, k, part] for k in range(4)]
                for row, conv in ((2 * i, m0 + 0.5 * (m1 + m2)), (2 * i + 1, 0.5 * (m1 - m2) - m3)):
                    value = own[f, row].astype(F32) + conv + bias[...]
                    own[f, row] = value.astype(jnp.bfloat16)
                return 0

            lax.fori_loop(0, rows // 2, finish, 0)
            pltpu.make_async_copy(own.at[f], out.at[f], out_sem.at[f]).start()

    for side, has in row_recvs:
        pl.when(has)(lambda side=side: rim_copy(2, side).wait_recv())
    for f in range(frames):
        put_frame(f + 2, own, f)

    pairs = [(f, t) for f in range(frames) for t in (2, 1, 0)]
    order = sorted(pairs, key=lambda p: (max(0, 2 - p[0] - p[1]), -p[1], -p[0]))
    left = {f: 3 for f in range(frames)}
    ready = 0
    for f, t in order:
        need = max(0, 2 - f - t)
        while ready < need:
            ready += 1
            slot = 2 - ready

            @pl.when(has_prev)
            def _():
                frame_copy(slot).wait_recv()
                if ready == 1:
                    for side, has in row_recvs:
                        pl.when(has)(lambda side=side: rim_copy(0, side).wait_recv())
                put_frame(slot, prev, slot)

        left[f] -= 1
        multiply(f, t, left[f] == 2, left[f] == 0)

    for side, has in row_sends:
        pl.when(has)(lambda side=side: rim_copy(2, side).wait_send())
        pl.when(has & has_next)(lambda side=side: rim_copy(0, side).wait_send())
    for slot in range(2):
        pl.when(has_next)(lambda slot=slot: frame_copy(slot).wait_send())
    for f in range(frames):
        pltpu.make_async_copy(own.at[f], out.at[f], out_sem.at[f]).wait()


def copy_kernel(source, target, sems):
    frames, rows = source.shape[:2]

    def each(act):
        for f in range(frames):
            for i in range(rows):
                act(pltpu.make_async_copy(source.at[f, i], target.at[f, i], sems.at[f, i]))

    each(lambda copy: copy.start())
    each(lambda copy: copy.wait())


def solution(mesh):
    sizes = (mesh.shape["req"], mesh.shape["tile"], mesh.shape["span"])
    reqs_n, tiles, spans = sizes

    def step(latents, frame_counts, norm_gain, norm_shift, conv_weight, conv_bias):
        frames, rows, cols, channels = latents.shape
        taps = conv_weight.shape[1] * conv_weight.shape[2]
        lines = -(-2 * frame_counts.shape[0] // 8) * 8
        members = tiles * spans
        bf16, dma = jnp.bfloat16, pltpu.SemaphoreType.DMA
        weight = conv_weight.reshape(9, 3 * channels, channels)
        whole = pl.BlockSpec(memory_space=pltpu.VMEM)
        anywhere = pl.BlockSpec(memory_space=pl.ANY)
        positions = frames * rows * cols
        result = pl.pallas_call(
            functools.partial(kernel, sizes),
            out_shape=jax.ShapeDtypeStruct(latents.shape, bf16),
            in_specs=[
                pl.BlockSpec(memory_space=pltpu.SMEM),
                anywhere,
                whole,
                whole,
                whole,
                anywhere,
            ],
            out_specs=anywhere,
            scratch_shapes=[
                pltpu.VMEM((frames, rows, cols, channels), bf16),
                pltpu.VMEM((2, rows, cols, channels), bf16),
                pltpu.VMEM((2, frames + 2, cols, channels), bf16),
                pltpu.VMEM((12, 3 * channels, channels), bf16),
                pltpu.VMEM((rows + 2, cols, 3 * channels), bf16),
                pltpu.VMEM((frames + 2, 4, rows // 2, cols, 3 * channels), bf16),
                pltpu.VMEM((frames, 4, rows // 2 * cols, channels), F32),
                pltpu.VMEM((lines, 128), F32),
                pltpu.VMEM((members, lines, 128), F32),
                pltpu.VMEM((reqs_n, lines, 128), F32),
                pltpu.VMEM((lines, channels), F32),
                dma((frames,)),
                dma((9,)),
                dma((frames,)),
                dma((members,)),
                dma((members,)),
                dma((reqs_n,)),
                dma((reqs_n,)),
                dma((2, 2)),
                dma((2, 2)),
                dma((2,)),
                dma((2,)),
            ],
            compiler_params=pltpu.CompilerParams(
                collective_id=0, has_side_effects=True, vmem_limit_bytes=62 * 1024 * 1024
            ),
            cost_estimate=pl.CostEstimate(
                flops=2 * positions * 2 * taps * channels * channels,
                bytes_accessed=2 * 3 * taps * channels * channels + 4 * positions * channels,
                transcendentals=2 * positions * channels,
            ),
        )(
            frame_counts,
            latents,
            norm_gain.reshape(1, channels),
            norm_shift.reshape(1, channels),
            conv_bias.reshape(1, channels),
            weight,
        )
        return pl.pallas_call(
            copy_kernel,
            out_shape=jax.ShapeDtypeStruct(latents.shape, bf16),
            in_specs=[anywhere],
            out_specs=anywhere,
            scratch_shapes=[dma((frames, rows))],
        )(result)

    placed = (P(("req", "span"), "tile", None, None), P(), P(), P(), P(), P())
    return jax.shard_map(
        step,
        mesh=mesh,
        in_specs=placed,
        out_specs=P(("req", "span"), "tile", None, None),
        check_vma=False,
    )
```

```python
import functools

import jax
import jax.numpy as jnp
from jax import lax
from jax.experimental import pallas as pl
from jax.experimental.pallas import tpu as pltpu
from jax.sharding import PartitionSpec as P

GROUPS = 32
EPSILON = 1e-06
MESH = pl.DeviceIdType.MESH
HIGHEST = lax.Precision.HIGHEST
F32 = jnp.float32


def kernel(
    sizes,
    counts,
    lat,
    gain,
    shift,
    bias,
    weight,
    out,
    own,
    prev,
    rim,
    wv,
    hid,
    acc,
    msg,
    stat_a,
    stat_b,
    table,
    own_sem,
    w_sem,
    out_sem,
    a_send,
    a_recv,
    b_send,
    b_recv,
    rim_send,
    rim_recv,
    frame_send,
    frame_recv,
):
    reqs_n, tiles, spans = sizes
    frames, rows, cols, channels = own.shape
    per_group = channels // GROUPS
    requests = counts.shape[0]
    req, tile, span = (lax.axis_index("req"), lax.axis_index("tile"), lax.axis_index("span"))
    place = req * spans + span
    places = reqs_n * spans
    has_next, has_prev = place < places - 1, place > 0
    has_up, has_down = tile > 0, tile < tiles - 1

    def at(chain, row):
        return {"req": chain // spans, "tile": row, "span": chain % spans}

    def chain_to(by):
        return jnp.clip(place + by, 0, places - 1)

    members_a = tiles * spans
    me_a = tile * spans + span

    def partner_a(k):
        other = (me_a + k) % members_a
        return {"req": req, "tile": other // spans, "span": other % spans}

    def partner_b(k):
        return {"req": (req + k) % reqs_n, "tile": tile, "span": span}

    for f in range(frames):
        pltpu.make_async_copy(lat.at[f], own.at[f], own_sem.at[f]).start()

    barrier = pltpu.get_barrier_semaphore()
    for k in range(1, members_a):
        pl.semaphore_signal(barrier, inc=1, device_id=partner_a(k), device_id_type=MESH)
    for k in range(1, reqs_n):
        pl.semaphore_signal(barrier, inc=1, device_id=partner_b(k), device_id_type=MESH)
    for by, has in ((1, has_next), (-1, has_prev)):

        @pl.when(has)
        def _():
            pl.semaphore_signal(
                barrier, inc=1, device_id=at(chain_to(by), tile), device_id_type=MESH
            )

        for step, has_row in ((-1, has_up), (1, has_down)):

            @pl.when(has & has_row)
            def _():
                pl.semaphore_signal(
                    barrier,
                    inc=1,
                    device_id=at(chain_to(by), jnp.clip(tile + step, 0, tiles - 1)),
                    device_id_type=MESH,
                )

    for t in (2, 1, 0):
        for b in range(3):
            i = 3 * t + b
            pltpu.make_async_copy(weight.at[i], wv.at[i], w_sem.at[i]).start()

    start_of, end_of, total = [], [], jnp.int32(0)
    for r in range(requests):
        start_of.append(total)
        total = total + counts[r]
        end_of.append(total)
    first = place * frames

    def member(slot, r):
        position = first + slot - 2
        return (position >= start_of[r]) & (position < end_of[r])

    def start_at(slot):
        found = jnp.int32(0)
        for r in range(requests):
            found = jnp.where(member(slot, r), start_of[r], found)
        return found

    per_frame = []
    for f in range(frames):
        pltpu.make_async_copy(lat.at[f], own.at[f], own_sem.at[f]).wait()

        def add_row(i, carry):
            s, q = carry
            x = own[f, i].astype(F32).reshape(cols // 8, 8, channels)
            return (s + jnp.sum(x, axis=0), q + jnp.sum(x * x, axis=0))

        zero = jnp.zeros((8, channels), F32)
        s, q = lax.fori_loop(0, rows, add_row, (zero, zero))
        per_frame.append((jnp.sum(s, axis=0, keepdims=True), jnp.sum(q, axis=0, keepdims=True)))
    table[...] = jnp.zeros_like(table)
    for r in range(requests):
        for which in range(2):
            line = jnp.zeros((1, channels), F32)
            for f in range(frames):
                line = line + jnp.where(member(f + 2, r), per_frame[f][which], 0.0)
            table[which * requests + r : which * requests + r + 1, :] = line
    lanes = msg.shape[1]
    to_group = (
        lax.broadcasted_iota(jnp.int32, (channels, lanes), 0) // per_group
        == lax.broadcasted_iota(jnp.int32, (channels, lanes), 1)
    ).astype(F32)
    from_group = (
        lax.broadcasted_iota(jnp.int32, (lanes, channels), 1) // per_group
        == lax.broadcasted_iota(jnp.int32, (lanes, channels), 0)
    ).astype(F32)
    msg[...] = jnp.dot(table[...], to_group, precision=HIGHEST, preferred_element_type=F32)
    stat_a[me_a] = msg[...]

    near = has_up.astype(jnp.int32) + has_down.astype(jnp.int32)
    sides = has_next.astype(jnp.int32) + has_prev.astype(jnp.int32)
    pl.semaphore_wait(barrier, members_a - 1 + reqs_n - 1 + sides * (1 + near))

    def copy_a(k):
        return pltpu.make_async_remote_copy(
            src_ref=msg,
            dst_ref=stat_a.at[me_a],
            send_sem=a_send.at[k],
            recv_sem=a_recv.at[me_a],
            device_id=partner_a(k),
            device_id_type=MESH,
        )

    def copy_b(k):
        return pltpu.make_async_remote_copy(
            src_ref=table.at[:, 0:lanes],
            dst_ref=stat_b.at[req],
            send_sem=b_send.at[k],
            recv_sem=b_recv.at[req],
            device_id=partner_b(k),
            device_id_type=MESH,
        )

    def rim_copy(slot, side):
        edge = rows - 1 if side == 0 else 0
        row_to = jnp.clip(tile + (1 if side == 0 else -1), 0, tiles - 1)
        forward = slot == 0
        source = lat.at[frames - 2 : frames, edge] if forward else lat.at[:, edge]
        count = 2 if forward else frames
        return pltpu.make_async_remote_copy(
            src_ref=source,
            dst_ref=rim.at[side, slot : slot + count],
            send_sem=rim_send.at[side, slot // 2],
            recv_sem=rim_recv.at[side, slot // 2],
            device_id=at(chain_to(1) if forward else place, row_to),
            device_id_type=MESH,
        )

    def frame_copy(slot):
        return pltpu.make_async_remote_copy(
            src_ref=lat.at[frames - 2 + slot],
            dst_ref=prev.at[slot],
            send_sem=frame_send.at[slot],
            recv_sem=frame_recv.at[slot],
            device_id=at(chain_to(1), tile),
            device_id_type=MESH,
        )

    row_sends = ((0, has_down), (1, has_up))
    row_recvs = ((0, has_up), (1, has_down))

    for k in range(1, members_a):
        copy_a(k).start()

    for k in range(1, members_a):
        copy_a(k).wait_send()
        other = (me_a + k) % members_a
        pltpu.make_async_remote_copy(
            src_ref=msg,
            dst_ref=stat_a.at[other],
            send_sem=a_send.at[k],
            recv_sem=a_recv.at[other],
            device_id=partner_a(k),
            device_id_type=MESH,
        ).wait_recv()
    part = jnp.sum(stat_a[...], axis=0)
    table[:, 0:lanes] = part
    stat_b[req] = part
    for k in range(1, reqs_n):
        copy_b(k).start()
    for side, has in row_sends:
        pl.when(has)(lambda side=side: rim_copy(2, side).start())
    pl.when(has_next)(lambda: frame_copy(1).start())
    for side, has in row_sends:
        pl.when(has & has_next)(lambda side=side: rim_copy(0, side).start())
    pl.when(has_next)(lambda: frame_copy(0).start())
    for k in range(1, reqs_n):
        copy_b(k).wait_send()
        other = (req + k) % reqs_n
        pltpu.make_async_remote_copy(
            src_ref=table.at[:, 0:lanes],
            dst_ref=stat_b.at[other],
            send_sem=b_send.at[k],
            recv_sem=b_recv.at[other],
            device_id=partner_b(k),
            device_id_type=MESH,
        ).wait_recv()
    whole = jnp.sum(stat_b[...], axis=0)
    cells = rows * tiles * cols * per_group
    lines = []
    for r in range(requests):
        n = jnp.full((1, lanes), counts[r] * cells, jnp.int32).astype(F32)
        mean = whole[r : r + 1] / n
        scale = lax.rsqrt(whole[requests + r : requests + r + 1] / n - mean * mean + EPSILON)
        lines.append((mean, scale))
    for r in range(requests):
        msg[r : r + 1, :] = lines[r][0]
        msg[requests + r : requests + r + 1, :] = lines[r][1]
    table[...] = jnp.dot(msg[...], from_group, precision=HIGHEST, preferred_element_type=F32)

    lane = min(128, channels)
    first_col = lax.broadcasted_iota(jnp.int32, (cols, lane), 0) == 0
    last_col = lax.broadcasted_iota(jnp.int32, (cols, lane), 0) == cols - 1

    def coefficients(slot):
        mean = jnp.zeros((1, channels), F32)
        scale = jnp.zeros((1, channels), F32)
        for r in range(requests):
            inside = member(slot, r)
            mean = jnp.where(inside, table[r : r + 1, :], mean)
            scale = jnp.where(inside, table[requests + r : requests + r + 1, :], scale)
        return mean, scale * gain[...] * 0.5, shift[...] * 0.5

    def put_row(slot, row, read, coef):
        mean, factor, offset = coef
        for c in range(0, channels, lane):
            part = slice(c, c + lane)
            x = read(part).astype(F32)
            h = (x - mean[:, part]) * factor[:, part] + offset[:, part]
            y = h + h * jnp.tanh(h)
            left = jnp.where(first_col, y, pltpu.roll(y, 1, 0))
            right = jnp.where(last_col, y, pltpu.roll(y, cols - 1, 0))
            hid[slot, row, :, c : c + lane] = left.astype(jnp.bfloat16)
            hid[slot, row, :, channels + c : channels + c + lane] = y.astype(jnp.bfloat16)
            hid[slot, row, :, 2 * channels + c : 2 * channels + c + lane] = right.astype(
                jnp.bfloat16
            )

    def put_frame(slot, source, index):
        coef = coefficients(slot)

        def body(i, _):
            put_row(slot, i + 1, lambda part: source[index, i, :, part], coef)
            return 0

        lax.fori_loop(0, rows, body, 0)
        for side, has in row_recvs:
            row = 0 if side == 0 else rows + 1
            edge = 0 if side == 0 else rows - 1

            @pl.when(has)
            def _():
                put_row(slot, row, lambda part: rim[side, slot, :, part], coef)

            @pl.when(jnp.logical_not(has))
            def _():
                hid[slot, row] = hid[slot, 1 + edge]

    def multiply(f, t, begin, end):
        source = jnp.maximum(first + f - 2 + t, start_at(f + 2)) - first + 2

        def body(b, _):
            if begin:
                i = 3 * t + b
                pltpu.make_async_copy(weight.at[i], wv.at[i], w_sem.at[i]).wait()
            lhs = hid[source, pl.ds(b, rows)].reshape(rows * cols, 3 * channels)
            acc[f] += jnp.dot(lhs, wv[3 * t + b], preferred_element_type=F32)
            return 0

        lax.fori_loop(0, 3, body, 0)
        if end:
            value = own[f].reshape(rows * cols, channels).astype(F32) + acc[f] + bias[...]
            own[f] = value.astype(jnp.bfloat16).reshape(rows, cols, channels)
            pltpu.make_async_copy(own.at[f], out.at[f], out_sem.at[f]).start()

    for side, has in row_recvs:
        pl.when(has)(lambda side=side: rim_copy(2, side).wait_recv())
    for f in range(frames):
        put_frame(f + 2, own, f)
    acc[...] = jnp.zeros_like(acc)

    pairs = [(f, t) for f in range(frames) for t in (2, 1, 0)]
    order = sorted(pairs, key=lambda p: (max(0, 2 - p[0] - p[1]), -p[1], -p[0]))
    seen, left = set(), {f: 3 for f in range(frames)}
    ready = 0
    for f, t in order:
        need = max(0, 2 - f - t)
        while ready < need:
            ready += 1
            slot = 2 - ready

            @pl.when(has_prev)
            def _():
                frame_copy(slot).wait_recv()
                if ready == 1:
                    for side, has in row_recvs:
                        pl.when(has)(lambda side=side: rim_copy(0, side).wait_recv())
                put_frame(slot, prev, slot)

        left[f] -= 1
        multiply(f, t, t not in seen, left[f] == 0)
        seen.add(t)

    for side, has in row_sends:
        pl.when(has)(lambda side=side: rim_copy(2, side).wait_send())
        pl.when(has & has_next)(lambda side=side: rim_copy(0, side).wait_send())
    for slot in range(2):
        pl.when(has_next)(lambda slot=slot: frame_copy(slot).wait_send())
    for f in range(frames):
        pltpu.make_async_copy(own.at[f], out.at[f], out_sem.at[f]).wait()


def copy_kernel(source, target, held, in_sems, out_sems):
    parts = held.shape[0]
    for i in range(parts):
        pltpu.make_async_copy(source.at[i], held.at[i], in_sems.at[i]).start()
    for i in range(parts):
        pltpu.make_async_copy(source.at[i], held.at[i], in_sems.at[i]).wait()
        pltpu.make_async_copy(held.at[i], target.at[i], out_sems.at[i]).start()
    for i in range(parts):
        pltpu.make_async_copy(held.at[i], target.at[i], out_sems.at[i]).wait()


def solution(mesh):
    sizes = (mesh.shape["req"], mesh.shape["tile"], mesh.shape["span"])
    reqs_n, tiles, spans = sizes

    def step(latents, frame_counts, norm_gain, norm_shift, conv_weight, conv_bias):
        frames, rows, cols, channels = latents.shape
        taps = conv_weight.shape[1] * conv_weight.shape[2]
        lines = -(-2 * frame_counts.shape[0] // 8) * 8
        members = tiles * spans
        bf16, dma = jnp.bfloat16, pltpu.SemaphoreType.DMA
        weight = conv_weight.reshape(9, 3 * channels, channels)
        whole = pl.BlockSpec(memory_space=pltpu.VMEM)
        anywhere = pl.BlockSpec(memory_space=pl.ANY)
        positions = frames * rows * cols
        result = pl.pallas_call(
            functools.partial(kernel, sizes),
            out_shape=jax.ShapeDtypeStruct(latents.shape, bf16),
            in_specs=[
                pl.BlockSpec(memory_space=pltpu.SMEM),
                anywhere,
                whole,
                whole,
                whole,
                anywhere,
            ],
            out_specs=anywhere,
            scratch_shapes=[
                pltpu.VMEM((frames, rows, cols, channels), bf16),
                pltpu.VMEM((2, rows, cols, channels), bf16),
                pltpu.VMEM((2, frames + 2, cols, channels), bf16),
                pltpu.VMEM((9, 3 * channels, channels), bf16),
                pltpu.VMEM((frames + 2, rows + 2, cols, 3 * channels), bf16),
                pltpu.VMEM((frames, rows * cols, channels), F32),
                pltpu.VMEM((lines, 128), F32),
                pltpu.VMEM((members, lines, 128), F32),
                pltpu.VMEM((reqs_n, lines, 128), F32),
                pltpu.VMEM((lines, channels), F32),
                dma((frames,)),
                dma((9,)),
                dma((frames,)),
                dma((members,)),
                dma((members,)),
                dma((reqs_n,)),
                dma((reqs_n,)),
                dma((2, 2)),
                dma((2, 2)),
                dma((2,)),
                dma((2,)),
            ],
            compiler_params=pltpu.CompilerParams(
                collective_id=0, has_side_effects=True, vmem_limit_bytes=56 * 1024 * 1024
            ),
            cost_estimate=pl.CostEstimate(
                flops=2 * positions * 3 * taps * channels * channels,
                bytes_accessed=2 * 3 * taps * channels * channels + 4 * positions * channels,
                transcendentals=2 * positions * channels,
            ),
        )(
            frame_counts,
            latents,
            norm_gain.reshape(1, channels),
            norm_shift.reshape(1, channels),
            conv_bias.reshape(1, channels),
            weight,
        )
        parts = (frames * rows // 2, 2, cols, channels)
        return pl.pallas_call(
            copy_kernel,
            out_shape=jax.ShapeDtypeStruct(parts, bf16),
            in_specs=[anywhere],
            out_specs=anywhere,
            scratch_shapes=[pltpu.VMEM(parts, bf16), dma((parts[0],)), dma((parts[0],))],
            compiler_params=pltpu.CompilerParams(vmem_limit_bytes=58 * 1024 * 1024),
        )(result.reshape(parts)).reshape(latents.shape)

    placed = (P(("req", "span"), "tile", None, None), P(), P(), P(), P(), P())
    return jax.shard_map(
        step,
        mesh=mesh,
        in_specs=placed,
        out_specs=P(("req", "span"), "tile", None, None),
        check_vma=False,
    )
```

```python
import functools

import jax
import jax.numpy as jnp
from jax import lax
from jax.experimental import pallas as pl
from jax.experimental.pallas import tpu as pltpu
from jax.sharding import PartitionSpec as P

GROUPS = 32
EPSILON = 1e-06
MESH = pl.DeviceIdType.MESH
F32 = jnp.float32


def kernel(
    sizes,
    counts,
    lat,
    gain,
    shift,
    bias,
    weight,
    out,
    own,
    prev,
    rim,
    wv,
    hid,
    acc,
    msg,
    stat_a,
    stat_b,
    table,
    own_sem,
    w_sem,
    out_sem,
    a_send,
    a_recv,
    b_send,
    b_recv,
    rim_send,
    rim_recv,
    frame_send,
    frame_recv,
):
    reqs_n, tiles, spans = sizes
    frames, rows, cols, channels = own.shape
    per_group = channels // GROUPS
    requests = counts.shape[0]
    req, tile, span = (lax.axis_index("req"), lax.axis_index("tile"), lax.axis_index("span"))
    place = req * spans + span
    places = reqs_n * spans
    has_next, has_prev = place < places - 1, place > 0
    has_up, has_down = tile > 0, tile < tiles - 1

    def at(chain, row):
        return {"req": chain // spans, "tile": row, "span": chain % spans}

    def chain_to(by):
        return jnp.clip(place + by, 0, places - 1)

    members_a = tiles * spans
    me_a = tile * spans + span

    def partner_a(k):
        other = (me_a + k) % members_a
        return {"req": req, "tile": other // spans, "span": other % spans}

    def partner_b(k):
        return {"req": (req + k) % reqs_n, "tile": tile, "span": span}

    for f in range(frames):
        pltpu.make_async_copy(lat.at[f], own.at[f], own_sem.at[f]).start()

    barrier = pltpu.get_barrier_semaphore()
    for k in range(1, members_a):
        pl.semaphore_signal(barrier, inc=1, device_id=partner_a(k), device_id_type=MESH)
    for k in range(1, reqs_n):
        pl.semaphore_signal(barrier, inc=1, device_id=partner_b(k), device_id_type=MESH)
    for by, has in ((1, has_next), (-1, has_prev)):

        @pl.when(has)
        def _():
            pl.semaphore_signal(
                barrier, inc=1, device_id=at(chain_to(by), tile), device_id_type=MESH
            )

        for step, has_row in ((-1, has_up), (1, has_down)):

            @pl.when(has & has_row)
            def _():
                pl.semaphore_signal(
                    barrier,
                    inc=1,
                    device_id=at(chain_to(by), jnp.clip(tile + step, 0, tiles - 1)),
                    device_id_type=MESH,
                )

    for t in (2, 1, 0):
        for b in range(3):
            i = 3 * t + b
            pltpu.make_async_copy(weight.at[i], wv.at[i], w_sem.at[i]).start()

    start_of, end_of, total = [], [], jnp.int32(0)
    for r in range(requests):
        start_of.append(total)
        total = total + counts[r]
        end_of.append(total)
    first = place * frames

    def member(slot, r):
        position = first + slot - 2
        return (position >= start_of[r]) & (position < end_of[r])

    def start_at(slot):
        found = jnp.int32(0)
        for r in range(requests):
            found = jnp.where(member(slot, r), start_of[r], found)
        return found

    per_frame = []
    for f in range(frames):
        pltpu.make_async_copy(lat.at[f], own.at[f], own_sem.at[f]).wait()

        def add_row(i, carry):
            s, q = carry
            x = own[f, i].astype(F32).reshape(cols // 8, 8, channels)
            return (s + jnp.sum(x, axis=0), q + jnp.sum(x * x, axis=0))

        zero = jnp.zeros((8, channels), F32)
        s, q = lax.fori_loop(0, rows, add_row, (zero, zero))
        per_frame.append((jnp.sum(s, axis=0, keepdims=True), jnp.sum(q, axis=0, keepdims=True)))
    table[...] = jnp.zeros_like(table)
    for r in range(requests):
        for which in range(2):
            line = jnp.zeros((1, channels), F32)
            for f in range(frames):
                line = line + jnp.where(member(f + 2, r), per_frame[f][which], 0.0)
            table[which * requests + r : which * requests + r + 1, :] = line
    lanes = msg.shape[1]
    pieces = channels // lanes
    spot = lax.broadcasted_iota(jnp.int32, (msg.shape[0], lanes), 1)

    def spread_sum(x, width):
        k = 1
        while k < width:
            after, before = pltpu.roll(x, lanes - k, 1), pltpu.roll(x, k, 1)
            x = x + jnp.where((spot & k) == 0, after, before)
            k *= 2
        return x

    packed = jnp.zeros((msg.shape[0], lanes), F32)
    for v in range(pieces):
        group = spread_sum(table[:, v * lanes : (v + 1) * lanes], per_group)
        packed = jnp.where(spot % pieces == v, group, packed)
    msg[...] = packed
    stat_a[me_a] = msg[...]

    near = has_up.astype(jnp.int32) + has_down.astype(jnp.int32)
    sides = has_next.astype(jnp.int32) + has_prev.astype(jnp.int32)
    pl.semaphore_wait(barrier, members_a - 1 + reqs_n - 1 + sides * (1 + near))

    def copy_a(k):
        return pltpu.make_async_remote_copy(
            src_ref=msg,
            dst_ref=stat_a.at[me_a],
            send_sem=a_send.at[k],
            recv_sem=a_recv.at[me_a],
            device_id=partner_a(k),
            device_id_type=MESH,
        )

    def copy_b(k):
        return pltpu.make_async_remote_copy(
            src_ref=table.at[:, 0:lanes],
            dst_ref=stat_b.at[req],
            send_sem=b_send.at[k],
            recv_sem=b_recv.at[req],
            device_id=partner_b(k),
            device_id_type=MESH,
        )

    def rim_copy(slot, side):
        edge = rows - 1 if side == 0 else 0
        row_to = jnp.clip(tile + (1 if side == 0 else -1), 0, tiles - 1)
        forward = slot == 0
        source = lat.at[frames - 2 : frames, edge] if forward else lat.at[:, edge]
        count = 2 if forward else frames
        return pltpu.make_async_remote_copy(
            src_ref=source,
            dst_ref=rim.at[side, slot : slot + count],
            send_sem=rim_send.at[side, slot // 2],
            recv_sem=rim_recv.at[side, slot // 2],
            device_id=at(chain_to(1) if forward else place, row_to),
            device_id_type=MESH,
        )

    def frame_copy(slot):
        return pltpu.make_async_remote_copy(
            src_ref=lat.at[frames - 2 + slot],
            dst_ref=prev.at[slot],
            send_sem=frame_send.at[slot],
            recv_sem=frame_recv.at[slot],
            device_id=at(chain_to(1), tile),
            device_id_type=MESH,
        )

    row_sends = ((0, has_down), (1, has_up))
    row_recvs = ((0, has_up), (1, has_down))

    for k in range(1, members_a):
        copy_a(k).start()
    for side, has in row_sends:
        pl.when(has)(lambda side=side: rim_copy(2, side).start())

    for k in range(1, members_a):
        copy_a(k).wait_send()
        other = (me_a + k) % members_a
        pltpu.make_async_remote_copy(
            src_ref=msg,
            dst_ref=stat_a.at[other],
            send_sem=a_send.at[k],
            recv_sem=a_recv.at[other],
            device_id=partner_a(k),
            device_id_type=MESH,
        ).wait_recv()
    part = jnp.sum(stat_a[...], axis=0)
    table[:, 0:lanes] = part
    stat_b[req] = part
    for k in range(1, reqs_n):
        copy_b(k).start()
    pl.when(has_next)(lambda: frame_copy(1).start())
    for side, has in row_sends:
        pl.when(has & has_next)(lambda side=side: rim_copy(0, side).start())
    pl.when(has_next)(lambda: frame_copy(0).start())
    for k in range(1, reqs_n):
        copy_b(k).wait_send()
        other = (req + k) % reqs_n
        pltpu.make_async_remote_copy(
            src_ref=table.at[:, 0:lanes],
            dst_ref=stat_b.at[other],
            send_sem=b_send.at[k],
            recv_sem=b_recv.at[other],
            device_id=partner_b(k),
            device_id_type=MESH,
        ).wait_recv()
    whole = jnp.sum(stat_b[...], axis=0)
    cells = rows * tiles * cols * per_group
    lines = []
    for r in range(requests):
        n = jnp.full((1, lanes), counts[r] * cells, jnp.int32).astype(F32)
        mean = whole[r : r + 1] / n
        scale = lax.rsqrt(whole[requests + r : requests + r + 1] / n - mean * mean + EPSILON)
        lines.append((mean, scale))
    for r in range(requests):
        msg[r : r + 1, :] = lines[r][0]
        msg[requests + r : requests + r + 1, :] = lines[r][1]
    for v in range(pieces):
        chosen = jnp.where(spot % pieces == v, msg[...], 0.0)
        table[:, v * lanes : (v + 1) * lanes] = spread_sum(chosen, pieces)

    lane = min(128, channels)
    first_col = lax.broadcasted_iota(jnp.int32, (cols, lane), 0) == 0
    last_col = lax.broadcasted_iota(jnp.int32, (cols, lane), 0) == cols - 1

    def coefficients(slot):
        mean = jnp.zeros((1, channels), F32)
        scale = jnp.zeros((1, channels), F32)
        for r in range(requests):
            inside = member(slot, r)
            mean = jnp.where(inside, table[r : r + 1, :], mean)
            scale = jnp.where(inside, table[requests + r : requests + r + 1, :], scale)
        return mean, scale * gain[...] * 0.5, shift[...] * 0.5

    def put_row(slot, row, read, coef):
        mean, factor, offset = coef
        for c in range(0, channels, lane):
            part = slice(c, c + lane)
            x = read(part).astype(F32)
            h = (x - mean[:, part]) * factor[:, part] + offset[:, part]
            y = h + h * jnp.tanh(h)
            left = jnp.where(first_col, y, pltpu.roll(y, 1, 0))
            right = jnp.where(last_col, y, pltpu.roll(y, cols - 1, 0))
            hid[slot, row, :, c : c + lane] = left.astype(jnp.bfloat16)
            hid[slot, row, :, channels + c : channels + c + lane] = y.astype(jnp.bfloat16)
            hid[slot, row, :, 2 * channels + c : 2 * channels + c + lane] = right.astype(
                jnp.bfloat16
            )

    def put_inner(slot, source, index):
        coef = coefficients(slot)

        def body(i, _):
            put_row(slot, i + 1, lambda part: source[index, i, :, part], coef)
            return 0

        lax.fori_loop(0, rows, body, 0)

    def put_edges(slot):
        coef = coefficients(slot)
        for side, has in row_recvs:
            row = 0 if side == 0 else rows + 1
            edge = 0 if side == 0 else rows - 1

            @pl.when(has)
            def _():
                put_row(slot, row, lambda part: rim[side, slot, :, part], coef)

            @pl.when(jnp.logical_not(has))
            def _():
                hid[slot, row] = hid[slot, 1 + edge]

    def multiply(f, t, begin, opens, end):
        source = jnp.maximum(first + f - 2 + t, start_at(f + 2)) - first + 2

        def product(b):
            if begin:
                i = 3 * t + b
                pltpu.make_async_copy(weight.at[i], wv.at[i], w_sem.at[i]).wait()
            lhs = hid[source, pl.ds(b, rows)].reshape(rows * cols, 3 * channels)
            return jnp.dot(lhs, wv[3 * t + b], preferred_element_type=F32)

        def body(b, _):
            acc[f] += product(b)
            return 0

        if opens:
            acc[f] = product(0)
        lax.fori_loop(1 if opens else 0, 2 if end else 3, body, 0)
        if end:
            value = own[f].reshape(rows * cols, channels).astype(F32) + bias[...]
            value = value + (acc[f] + product(2))
            own[f] = value.astype(jnp.bfloat16).reshape(rows, cols, channels)
            pltpu.make_async_copy(own.at[f], out.at[f], out_sem.at[f]).start()

    for f in range(frames):
        put_inner(f + 2, own, f)
    for side, has in row_recvs:
        pl.when(has)(lambda side=side: rim_copy(2, side).wait_recv())
    for f in range(frames):
        put_edges(f + 2)

    pairs = [(f, t) for f in range(frames) for t in (2, 1, 0)]
    order = sorted(pairs, key=lambda p: (max(0, 2 - p[0] - p[1]), -p[1], -p[0]))
    seen, left = set(), {f: 3 for f in range(frames)}
    ready = 0
    for f, t in order:
        need = max(0, 2 - f - t)
        while ready < need:
            ready += 1
            slot = 2 - ready

            @pl.when(has_prev)
            def _():
                frame_copy(slot).wait_recv()
                if ready == 1:
                    for side, has in row_recvs:
                        pl.when(has)(lambda side=side: rim_copy(0, side).wait_recv())
                put_inner(slot, prev, slot)
                put_edges(slot)

        left[f] -= 1
        multiply(f, t, t not in seen, left[f] == 2, left[f] == 0)
        seen.add(t)

    for side, has in row_sends:
        pl.when(has)(lambda side=side: rim_copy(2, side).wait_send())
        pl.when(has & has_next)(lambda side=side: rim_copy(0, side).wait_send())
    for slot in range(2):
        pl.when(has_next)(lambda slot=slot: frame_copy(slot).wait_send())
    for f in range(frames):
        pltpu.make_async_copy(own.at[f], out.at[f], out_sem.at[f]).wait()


def copy_kernel(source, target, held, in_sems, out_sems):
    parts = held.shape[0]
    for i in range(parts):
        pltpu.make_async_copy(source.at[i], held.at[i], in_sems.at[i]).start()
    for i in range(parts):
        pltpu.make_async_copy(source.at[i], held.at[i], in_sems.at[i]).wait()
        pltpu.make_async_copy(held.at[i], target.at[i], out_sems.at[i]).start()
    for i in range(parts):
        pltpu.make_async_copy(held.at[i], target.at[i], out_sems.at[i]).wait()


def solution(mesh):
    sizes = (mesh.shape["req"], mesh.shape["tile"], mesh.shape["span"])
    reqs_n, tiles, spans = sizes

    def step(latents, frame_counts, norm_gain, norm_shift, conv_weight, conv_bias):
        frames, rows, cols, channels = latents.shape
        taps = conv_weight.shape[1] * conv_weight.shape[2]
        lines = -(-2 * frame_counts.shape[0] // 8) * 8
        members = tiles * spans
        bf16, dma = jnp.bfloat16, pltpu.SemaphoreType.DMA
        weight = conv_weight.reshape(9, 3 * channels, channels)
        whole = pl.BlockSpec(memory_space=pltpu.VMEM)
        anywhere = pl.BlockSpec(memory_space=pl.ANY)
        positions = frames * rows * cols
        result = pl.pallas_call(
            functools.partial(kernel, sizes),
            out_shape=jax.ShapeDtypeStruct(latents.shape, bf16),
            in_specs=[
                pl.BlockSpec(memory_space=pltpu.SMEM),
                anywhere,
                whole,
                whole,
                whole,
                anywhere,
            ],
            out_specs=anywhere,
            scratch_shapes=[
                pltpu.VMEM((frames, rows, cols, channels), bf16),
                pltpu.VMEM((2, rows, cols, channels), bf16),
                pltpu.VMEM((2, frames + 2, cols, channels), bf16),
                pltpu.VMEM((9, 3 * channels, channels), bf16),
                pltpu.VMEM((frames + 2, rows + 2, cols, 3 * channels), bf16),
                pltpu.VMEM((frames, rows * cols, channels), F32),
                pltpu.VMEM((lines, 128), F32),
                pltpu.VMEM((members, lines, 128), F32),
                pltpu.VMEM((reqs_n, lines, 128), F32),
                pltpu.VMEM((lines, channels), F32),
                dma((frames,)),
                dma((9,)),
                dma((frames,)),
                dma((members,)),
                dma((members,)),
                dma((reqs_n,)),
                dma((reqs_n,)),
                dma((2, 2)),
                dma((2, 2)),
                dma((2,)),
                dma((2,)),
            ],
            compiler_params=pltpu.CompilerParams(
                collective_id=0, has_side_effects=True, vmem_limit_bytes=56 * 1024 * 1024
            ),
            cost_estimate=pl.CostEstimate(
                flops=2 * positions * 3 * taps * channels * channels,
                bytes_accessed=2 * 3 * taps * channels * channels + 4 * positions * channels,
                transcendentals=2 * positions * channels,
            ),
        )(
            frame_counts,
            latents,
            norm_gain.reshape(1, channels),
            norm_shift.reshape(1, channels),
            conv_bias.reshape(1, channels),
            weight,
        )
        parts = (frames * rows // 2, 2, cols, channels)
        return pl.pallas_call(
            copy_kernel,
            out_shape=jax.ShapeDtypeStruct(parts, bf16),
            in_specs=[anywhere],
            out_specs=anywhere,
            scratch_shapes=[pltpu.VMEM(parts, bf16), dma((parts[0],)), dma((parts[0],))],
            compiler_params=pltpu.CompilerParams(vmem_limit_bytes=58 * 1024 * 1024),
        )(result.reshape(parts)).reshape(latents.shape)

    placed = (P(("req", "span"), "tile", None, None), P(), P(), P(), P(), P())
    return jax.shard_map(
        step,
        mesh=mesh,
        in_specs=placed,
        out_specs=P(("req", "span"), "tile", None, None),
        check_vma=False,
    )
```

```python
import functools

import jax
import jax.numpy as jnp
from jax import lax
from jax.experimental import pallas as pl
from jax.experimental.pallas import tpu as pltpu
from jax.sharding import PartitionSpec as P

GROUPS = 32
EPSILON = 1e-06
MESH = pl.DeviceIdType.MESH
F32 = jnp.float32


def kernel(
    sizes,
    counts,
    lat,
    gain,
    shift,
    bias,
    weight,
    out,
    own,
    prev,
    rim,
    wv,
    hid,
    acc,
    msg,
    stat_a,
    stat_b,
    table,
    own_sem,
    w_sem,
    out_sem,
    a_send,
    a_recv,
    b_send,
    b_recv,
    rim_send,
    rim_recv,
    frame_send,
    frame_recv,
):
    reqs_n, tiles, spans = sizes
    frames, rows, cols, channels = own.shape
    per_group = channels // GROUPS
    requests = counts.shape[0]
    req, tile, span = (lax.axis_index("req"), lax.axis_index("tile"), lax.axis_index("span"))
    place = req * spans + span
    places = reqs_n * spans
    has_next, has_prev = place < places - 1, place > 0
    has_up, has_down = tile > 0, tile < tiles - 1

    def at(chain, row):
        return {"req": chain // spans, "tile": row, "span": chain % spans}

    def chain_to(by):
        return jnp.clip(place + by, 0, places - 1)

    members_a = tiles * spans
    me_a = tile * spans + span

    def partner_a(k):
        other = (me_a + k) % members_a
        return {"req": req, "tile": other // spans, "span": other % spans}

    def partner_b(k):
        return {"req": (req + k) % reqs_n, "tile": tile, "span": span}

    for f in range(frames):
        pltpu.make_async_copy(lat.at[f], own.at[f], own_sem.at[f]).start()

    barrier = pltpu.get_barrier_semaphore()
    for k in range(1, members_a):
        pl.semaphore_signal(barrier, inc=1, device_id=partner_a(k), device_id_type=MESH)
    for k in range(1, reqs_n):
        pl.semaphore_signal(barrier, inc=1, device_id=partner_b(k), device_id_type=MESH)
    for by, has in ((1, has_next), (-1, has_prev)):

        @pl.when(has)
        def _():
            pl.semaphore_signal(
                barrier, inc=1, device_id=at(chain_to(by), tile), device_id_type=MESH
            )

        for step, has_row in ((-1, has_up), (1, has_down)):

            @pl.when(has & has_row)
            def _():
                pl.semaphore_signal(
                    barrier,
                    inc=1,
                    device_id=at(chain_to(by), jnp.clip(tile + step, 0, tiles - 1)),
                    device_id_type=MESH,
                )

    def load_weights(t):
        for i in range(3 * t, 3 * t + 3):
            pltpu.make_async_copy(weight.at[i], wv.at[i], w_sem.at[i]).start()

    start_of, end_of, total = [], [], jnp.int32(0)
    for r in range(requests):
        start_of.append(total)
        total = total + counts[r]
        end_of.append(total)
    first = place * frames

    def member(slot, r):
        position = first + slot - 2
        return (position >= start_of[r]) & (position < end_of[r])

    def start_at(slot):
        found = jnp.int32(0)
        for r in range(requests):
            found = jnp.where(member(slot, r), start_of[r], found)
        return found

    per_frame = []
    for f in range(frames):
        pltpu.make_async_copy(lat.at[f], own.at[f], own_sem.at[f]).wait()

        def add_row(i, carry):
            s, q = carry
            x = own[f, i].astype(F32).reshape(cols // 8, 8, channels)
            return (s + jnp.sum(x, axis=0), q + jnp.sum(x * x, axis=0))

        zero = jnp.zeros((8, channels), F32)
        s, q = lax.fori_loop(0, rows, add_row, (zero, zero))
        per_frame.append((jnp.sum(s, axis=0, keepdims=True), jnp.sum(q, axis=0, keepdims=True)))
    table[...] = jnp.zeros_like(table)
    for r in range(requests):
        for which in range(2):
            line = jnp.zeros((1, channels), F32)
            for f in range(frames):
                line = line + jnp.where(member(f + 2, r), per_frame[f][which], 0.0)
            table[which * requests + r : which * requests + r + 1, :] = line
    lanes = msg.shape[1]
    pieces = channels // lanes
    spot = lax.broadcasted_iota(jnp.int32, (msg.shape[0], lanes), 1)

    def spread_sum(x, width):
        k = 1
        while k < width:
            after, before = pltpu.roll(x, lanes - k, 1), pltpu.roll(x, k, 1)
            x = x + jnp.where((spot & k) == 0, after, before)
            k *= 2
        return x

    packed = jnp.zeros((msg.shape[0], lanes), F32)
    for v in range(pieces):
        group = spread_sum(table[:, v * lanes : (v + 1) * lanes], per_group)
        packed = jnp.where(spot % pieces == v, group, packed)
    msg[...] = packed
    stat_a[me_a] = msg[...]

    near = has_up.astype(jnp.int32) + has_down.astype(jnp.int32)
    sides = has_next.astype(jnp.int32) + has_prev.astype(jnp.int32)
    pl.semaphore_wait(barrier, members_a - 1 + reqs_n - 1 + sides * (1 + near))

    def copy_a(k):
        return pltpu.make_async_remote_copy(
            src_ref=msg,
            dst_ref=stat_a.at[me_a],
            send_sem=a_send.at[k],
            recv_sem=a_recv.at[me_a],
            device_id=partner_a(k),
            device_id_type=MESH,
        )

    def copy_b(k):
        return pltpu.make_async_remote_copy(
            src_ref=table.at[:, 0:lanes],
            dst_ref=stat_b.at[req],
            send_sem=b_send.at[k],
            recv_sem=b_recv.at[req],
            device_id=partner_b(k),
            device_id_type=MESH,
        )

    def rim_copy(slot, side):
        edge = rows - 1 if side == 0 else 0
        row_to = jnp.clip(tile + (1 if side == 0 else -1), 0, tiles - 1)
        forward = slot == 0
        source = lat.at[frames - 2 : frames, edge] if forward else lat.at[:, edge]
        count = 2 if forward else frames
        return pltpu.make_async_remote_copy(
            src_ref=source,
            dst_ref=rim.at[side, slot : slot + count],
            send_sem=rim_send.at[side, slot // 2],
            recv_sem=rim_recv.at[side, slot // 2],
            device_id=at(chain_to(1) if forward else place, row_to),
            device_id_type=MESH,
        )

    def frame_copy(slot):
        return pltpu.make_async_remote_copy(
            src_ref=lat.at[frames - 2 + slot],
            dst_ref=prev.at[slot],
            send_sem=frame_send.at[slot],
            recv_sem=frame_recv.at[slot],
            device_id=at(chain_to(1), tile),
            device_id_type=MESH,
        )

    row_sends = ((0, has_down), (1, has_up))
    row_recvs = ((0, has_up), (1, has_down))

    for k in range(1, members_a):
        copy_a(k).start()
    for side, has in row_sends:
        pl.when(has)(lambda side=side: rim_copy(2, side).start())

    for k in range(1, members_a):
        copy_a(k).wait_send()
        other = (me_a + k) % members_a
        pltpu.make_async_remote_copy(
            src_ref=msg,
            dst_ref=stat_a.at[other],
            send_sem=a_send.at[k],
            recv_sem=a_recv.at[other],
            device_id=partner_a(k),
            device_id_type=MESH,
        ).wait_recv()
    part = jnp.sum(stat_a[...], axis=0)
    table[:, 0:lanes] = part
    stat_b[req] = part
    for k in range(1, reqs_n):
        copy_b(k).start()
    load_weights(2)
    load_weights(1)
    pl.when(has_next)(lambda: frame_copy(1).start())
    for side, has in row_sends:
        pl.when(has & has_next)(lambda side=side: rim_copy(0, side).start())
    pl.when(has_next)(lambda: frame_copy(0).start())
    load_weights(0)
    for k in range(1, reqs_n):
        copy_b(k).wait_send()
        other = (req + k) % reqs_n
        pltpu.make_async_remote_copy(
            src_ref=table.at[:, 0:lanes],
            dst_ref=stat_b.at[other],
            send_sem=b_send.at[k],
            recv_sem=b_recv.at[other],
            device_id=partner_b(k),
            device_id_type=MESH,
        ).wait_recv()
    whole = jnp.sum(stat_b[...], axis=0)
    cells = rows * tiles * cols * per_group
    lines = []
    for r in range(requests):
        n = jnp.full((1, lanes), counts[r] * cells, jnp.int32).astype(F32)
        mean = whole[r : r + 1] / n
        scale = lax.rsqrt(whole[requests + r : requests + r + 1] / n - mean * mean + EPSILON)
        lines.append((mean, scale))
    for r in range(requests):
        msg[r : r + 1, :] = lines[r][0]
        msg[requests + r : requests + r + 1, :] = lines[r][1]
    for v in range(pieces):
        chosen = jnp.where(spot % pieces == v, msg[...], 0.0)
        table[:, v * lanes : (v + 1) * lanes] = spread_sum(chosen, pieces)

    lane = min(128, channels)
    first_col = lax.broadcasted_iota(jnp.int32, (cols, lane), 0) == 0
    last_col = lax.broadcasted_iota(jnp.int32, (cols, lane), 0) == cols - 1

    def coefficients(slot):
        mean = jnp.zeros((1, channels), F32)
        scale = jnp.zeros((1, channels), F32)
        for r in range(requests):
            inside = member(slot, r)
            mean = jnp.where(inside, table[r : r + 1, :], mean)
            scale = jnp.where(inside, table[requests + r : requests + r + 1, :], scale)
        return mean, scale * gain[...] * 0.5, shift[...] * 0.5

    def put_row(slot, row, read, coef):
        mean, factor, offset = coef
        for c in range(0, channels, lane):
            part = slice(c, c + lane)
            x = read(part).astype(F32)
            h = (x - mean[:, part]) * factor[:, part] + offset[:, part]
            y = h + h * jnp.tanh(h)
            left = jnp.where(first_col, y, pltpu.roll(y, 1, 0))
            right = jnp.where(last_col, y, pltpu.roll(y, cols - 1, 0))
            hid[slot, row, :, c : c + lane] = left.astype(jnp.bfloat16)
            hid[slot, row, :, channels + c : channels + c + lane] = y.astype(jnp.bfloat16)
            hid[slot, row, :, 2 * channels + c : 2 * channels + c + lane] = right.astype(
                jnp.bfloat16
            )

    def put_inner(slot, source, index):
        coef = coefficients(slot)

        def body(i, _):
            put_row(slot, i + 1, lambda part: source[index, i, :, part], coef)
            return 0

        lax.fori_loop(0, rows, body, 0)

    def put_edges(slot):
        coef = coefficients(slot)
        for side, has in row_recvs:
            row = 0 if side == 0 else rows + 1
            edge = 0 if side == 0 else rows - 1

            @pl.when(has)
            def _():
                put_row(slot, row, lambda part: rim[side, slot, :, part], coef)

            @pl.when(jnp.logical_not(has))
            def _():
                hid[slot, row] = hid[slot, 1 + edge]

    def multiply(f, t, begin, opens, end):
        source = jnp.maximum(first + f - 2 + t, start_at(f + 2)) - first + 2

        def product(b):
            if begin:
                i = 3 * t + b
                pltpu.make_async_copy(weight.at[i], wv.at[i], w_sem.at[i]).wait()
            lhs = hid[source, pl.ds(b, rows)].reshape(rows * cols, 3 * channels)
            return jnp.dot(lhs, wv[3 * t + b], preferred_element_type=F32)

        def body(b, _):
            acc[f] += product(b)
            return 0

        if opens:
            acc[f] = product(0)
        lax.fori_loop(1 if opens else 0, 2 if end else 3, body, 0)
        if end:
            value = own[f].reshape(rows * cols, channels).astype(F32) + bias[...]
            value = value + (acc[f] + product(2))
            own[f] = value.astype(jnp.bfloat16).reshape(rows, cols, channels)
            pltpu.make_async_copy(own.at[f], out.at[f], out_sem.at[f]).start()

    for f in range(frames):
        put_inner(f + 2, own, f)
    for side, has in row_recvs:
        pl.when(has)(lambda side=side: rim_copy(2, side).wait_recv())
    for f in range(frames):
        put_edges(f + 2)

    pairs = [(f, t) for f in range(frames) for t in (2, 1, 0)]
    order = sorted(pairs, key=lambda p: (max(0, 2 - p[0] - p[1]), -p[1], -p[0]))
    seen, left = set(), {f: 3 for f in range(frames)}
    ready = 0
    for f, t in order:
        need = max(0, 2 - f - t)
        while ready < need:
            ready += 1
            slot = 2 - ready

            @pl.when(has_prev)
            def _():
                frame_copy(slot).wait_recv()
                if ready == 1:
                    for side, has in row_recvs:
                        pl.when(has)(lambda side=side: rim_copy(0, side).wait_recv())
                put_inner(slot, prev, slot)
                put_edges(slot)

        left[f] -= 1
        multiply(f, t, t not in seen, left[f] == 2, left[f] == 0)
        seen.add(t)

    for side, has in row_sends:
        pl.when(has)(lambda side=side: rim_copy(2, side).wait_send())
        pl.when(has & has_next)(lambda side=side: rim_copy(0, side).wait_send())
    for slot in range(2):
        pl.when(has_next)(lambda slot=slot: frame_copy(slot).wait_send())
    for f in range(frames):
        pltpu.make_async_copy(own.at[f], out.at[f], out_sem.at[f]).wait()


def copy_kernel(source, target, held, in_sems, out_sems):
    parts = held.shape[0]
    for i in range(parts):
        pltpu.make_async_copy(source.at[i], held.at[i], in_sems.at[i]).start()
    for i in range(parts):
        pltpu.make_async_copy(source.at[i], held.at[i], in_sems.at[i]).wait()
        pltpu.make_async_copy(held.at[i], target.at[i], out_sems.at[i]).start()
    for i in range(parts):
        pltpu.make_async_copy(held.at[i], target.at[i], out_sems.at[i]).wait()


def solution(mesh):
    sizes = (mesh.shape["req"], mesh.shape["tile"], mesh.shape["span"])
    reqs_n, tiles, spans = sizes

    def step(latents, frame_counts, norm_gain, norm_shift, conv_weight, conv_bias):
        frames, rows, cols, channels = latents.shape
        taps = conv_weight.shape[1] * conv_weight.shape[2]
        lines = -(-2 * frame_counts.shape[0] // 8) * 8
        members = tiles * spans
        bf16, dma = jnp.bfloat16, pltpu.SemaphoreType.DMA
        weight = conv_weight.reshape(9, 3 * channels, channels)
        whole = pl.BlockSpec(memory_space=pltpu.VMEM)
        anywhere = pl.BlockSpec(memory_space=pl.ANY)
        positions = frames * rows * cols
        result = pl.pallas_call(
            functools.partial(kernel, sizes),
            out_shape=jax.ShapeDtypeStruct(latents.shape, bf16),
            in_specs=[
                pl.BlockSpec(memory_space=pltpu.SMEM),
                anywhere,
                whole,
                whole,
                whole,
                anywhere,
            ],
            out_specs=anywhere,
            scratch_shapes=[
                pltpu.VMEM((frames, rows, cols, channels), bf16),
                pltpu.VMEM((2, rows, cols, channels), bf16),
                pltpu.VMEM((2, frames + 2, cols, channels), bf16),
                pltpu.VMEM((9, 3 * channels, channels), bf16),
                pltpu.VMEM((frames + 2, rows + 2, cols, 3 * channels), bf16),
                pltpu.VMEM((frames, rows * cols, channels), F32),
                pltpu.VMEM((lines, 128), F32),
                pltpu.VMEM((members, lines, 128), F32),
                pltpu.VMEM((reqs_n, lines, 128), F32),
                pltpu.VMEM((lines, channels), F32),
                dma((frames,)),
                dma((9,)),
                dma((frames,)),
                dma((members,)),
                dma((members,)),
                dma((reqs_n,)),
                dma((reqs_n,)),
                dma((2, 2)),
                dma((2, 2)),
                dma((2,)),
                dma((2,)),
            ],
            compiler_params=pltpu.CompilerParams(
                collective_id=0, has_side_effects=True, vmem_limit_bytes=56 * 1024 * 1024
            ),
            cost_estimate=pl.CostEstimate(
                flops=2 * positions * 3 * taps * channels * channels,
                bytes_accessed=2 * 3 * taps * channels * channels + 4 * positions * channels,
                transcendentals=2 * positions * channels,
            ),
        )(
            frame_counts,
            latents,
            norm_gain.reshape(1, channels),
            norm_shift.reshape(1, channels),
            conv_bias.reshape(1, channels),
            weight,
        )
        parts = (frames * rows // 2, 2, cols, channels)
        return pl.pallas_call(
            copy_kernel,
            out_shape=jax.ShapeDtypeStruct(parts, bf16),
            in_specs=[anywhere],
            out_specs=anywhere,
            scratch_shapes=[pltpu.VMEM(parts, bf16), dma((parts[0],)), dma((parts[0],))],
            compiler_params=pltpu.CompilerParams(vmem_limit_bytes=58 * 1024 * 1024),
        )(result.reshape(parts)).reshape(latents.shape)

    placed = (P(("req", "span"), "tile", None, None), P(), P(), P(), P(), P())
    return jax.shard_map(
        step,
        mesh=mesh,
        in_specs=placed,
        out_specs=P(("req", "span"), "tile", None, None),
        check_vma=False,
    )
```
